1024 devices in a mesh: pipe: 16 (over y, core), expert: 64 (over z, x).
Axes of the slice: x: 8, y: 8, z: 8, core: 2. Of those that a mesh axis runs over, the one named last changes fastest.
Arguments:
- tokens: bfloat16 [8192, 3584], P('expert', 'pipe'), may hold values from -170 to 170
- routes: int32 [8192, 2], P('expert'), may hold values from 0 to 63, all different within a row; in each aligned block of 128 rows (0 to 127, 128 to 255, ...) at most 5 rows name the same one
- router: bfloat16 [3584, 64], P('pipe'), may hold values from -0.09375 to 0.09375
- w_gate: bfloat16 [64, 3584, 2048], P('expert', None, 'pipe'), may hold values from -0.09375 to 0.09375
- w_up: bfloat16 [64, 3584, 2048], P('expert', None, 'pipe'), may hold values from -0.09375 to 0.09375
- w_down: bfloat16 [64, 2048, 3584], P('expert', 'pipe'), may hold values from -0.125 to 0.125
Outputs:
- mixed: bfloat16 [8192, 3584], P('expert', 'pipe')
The draws below stay inside these ranges and needn't reach their ends.
Inputs may be any that keep to these rules, and one draw needn't show every extreme that they name: `routes`: each row names 2 different experts; among the 128 rows of one index of expert no expert is named more than 5 times.
All inputs are finite; a program needn't handle non-finite values.
Results may differ from the reference program's by a relative error of at most 0.024.
Values may be sent and summed in bfloat16 or wider, within the bound.
A program may use at most 32 MiB of HBM per device.

```python
import math
import jax
import jax.numpy as jnp
import numpy as np
from jax import lax

D = 3584
FF = 2048
TOPK = 2
TOK_DEV = 128
EXPERTS = 64
CAP = 5
TOKENS = 8192
N_PIPE = 16
N_EXPERT = 64


def draw_tokens(key, part):
    key = jax.random.fold_in(key, 11)
    first = jax.random.fold_in(key, 0)
    spot = jnp.arange(D, dtype=jnp.float32) / D
    column = jnp.power(3.0, spot)[None, :]
    values = jax.random.truncated_normal(first, -4.0, 4.0, (TOKENS, D), jnp.float32) * column
    return values.astype(jnp.bfloat16)


def block_levels(own_key, shape, shards, low, top_value):
    def one(axis_at, shards_of):
        heights = jax.random.uniform(jax.random.fold_in(jax.random.fold_in(own_key, 6), axis_at), (shards_of,), jnp.float32, low / len(shards), top_value / len(shards))
        return jnp.repeat(jnp.exp(heights), shape[axis_at] // shards_of).reshape((-1,) + (1,) * (len(shape) - axis_at - 1))

    loudness = one(*shards[0])
    for cut in shards[1:]:
        loudness = loudness * one(*cut)
    return loudness


def routed_block(key, own, number, rows, number_of, top, limit, slope):
    ranking = jax.random.permutation(key, number_of)
    heavy_load, common = shares(number_of, rows * top, limit, slope, True), shares(number_of, rows * top, limit, slope, False)
    places = jnp.arange(number_of)

    def named(lengths, turn):
        used = int((lengths > 0).sum())
        fixed = max(1, used // 4)
        passed = fixed + (places - fixed + turn * (used - fixed)) % max(1, number_of - fixed)
        return jnp.zeros((number_of,), jnp.int32).at[ranking[jnp.where(places < fixed, places, passed)]].set(jnp.asarray(lengths, jnp.int32))

    lengths = jnp.where(number % 4 == 0, named(heavy_load, number // 4), named(common, number - number // 4 - 1))
    mixed = jax.random.permutation(jax.random.fold_in(own, 3), number_of)
    donor, sink = mixed[0:number_of // 2 * 2:2], mixed[1:number_of // 2 * 2:2]
    margin = jnp.minimum(lengths[donor] - 1, limit - lengths[sink]) // 2
    margin = jnp.where((donor == ranking[0]) | (sink == ranking[0]) | (lengths[sink] == 0), 0, jnp.maximum(margin, 0))
    passed = jax.random.randint(jax.random.fold_in(own, 4), (number_of // 2,), 0, 1 << 20) % (margin + 1)
    lengths = lengths.at[donor].add(-passed).at[sink].add(passed)
    items = jnp.searchsorted(jnp.cumsum(lengths), jnp.arange(rows * top), side="right").astype(jnp.int32)
    grid = items.reshape(top, rows).T
    grid = grid[jax.random.permutation(jax.random.fold_in(own, 1), rows)]
    turn = jax.random.randint(jax.random.fold_in(own, 2), (rows, 1), 0, top)
    return jnp.take_along_axis(grid, (jnp.arange(top)[None, :] + turn) % top, axis=1)


def shares(count, total, reach, lean, full):
    portions = [(1 << 20) // math.isqrt(grade ** lean) + 1 for grade in range(1, count + 1)]
    largest = reach if full else min(reach, max(-(-total // count), total * portions[0] // sum(portions)))
    least = 1 if total - largest >= count - 1 else 0
    counts, rest = [largest] + [least] * (count - 1), total - largest - least * (count - 1)
    while rest > 0:
        free = [i for i in range(1, count) if counts[i] < largest] or [i for i in range(1, count) if counts[i] < reach]
        pool, left = sum([portions[i] for i in free]), rest
        for i in free:
            extra = min(reach - counts[i], max(1, left * portions[i] // pool), rest)
            counts[i] = counts[i] + extra
            rest = rest - extra
    return np.array(counts)


def bell_draw(stream_key, shape, spread, bound, cuts=(), kind=jnp.bfloat16):
    result = jax.random.normal(stream_key, shape, jnp.float32) * spread
    if len(cuts) > 0:
        result = block_levels(stream_key, shape, cuts, -0.22, 0.18) * result
    return jnp.clip(result, min=-bound, max=bound).astype(kind)


def setup_inputs(seed: int = 0) -> dict:
    key_of = jax.random.split(jax.random.key(seed), 7)
    tokens = draw_tokens(jax.random.fold_in(key_of[6], 71), 0)
    routes_keys = jax.random.split(jax.random.fold_in(key_of[1], 1), TOKENS // TOK_DEV)
    routes_turns = jax.random.permutation(jax.random.fold_in(key_of[1], 3), TOKENS // TOK_DEV)
    routes = jax.vmap(lambda own, number: routed_block(jax.random.fold_in(key_of[1], 2), own, number, TOK_DEV, EXPERTS, TOPK, CAP, 2))(routes_keys, routes_turns).reshape((TOKENS, TOPK))
    router = bell_draw(key_of[2], (D, EXPERTS), D ** -0.5, 0.09375, ((0, 16),))
    w_gate = bell_draw(key_of[3], (EXPERTS, D, FF), D ** -0.5, 0.09375, ((0, 64), (2, 16)))
    w_up = bell_draw(key_of[4], (EXPERTS, D, FF), D ** -0.5, 0.09375, ((0, 64), (2, 16)))
    w_down = bell_draw(key_of[5], (EXPERTS, FF, D), FF ** -0.5, 0.125, ((0, 64), (1, 16)))
    return dict(tokens=tokens, routes=routes, router=router, w_gate=w_gate, w_up=w_up, w_down=w_down)


eps = 1e-06

def reference(tokens, routes, router, w_gate, w_up, w_down):
    x = tokens.astype(jnp.float32)
    rstd = lax.rsqrt(lax.optimization_barrier(jnp.mean(x * x, axis=1)) + eps)
    logits = rstd[:, None] * jnp.dot(tokens, router, preferred_element_type=jnp.float32)
    chosen = jnp.take_along_axis(logits, routes, axis=1)
    score = jax.nn.sigmoid(chosen)
    weight = score / lax.optimization_barrier(jnp.sum(score, axis=1, keepdims=True))
    per_src = routes.reshape(N_EXPERT, TOK_DEV * TOPK)
    onehot = (per_src[:, :, None] == jnp.arange(EXPERTS, dtype=jnp.int32)[None, None, :]).astype(jnp.int32)
    position = jnp.cumsum(onehot, axis=1) - 1
    slot = jnp.take_along_axis(position, per_src[:, :, None], axis=2)[:, :, 0]
    total_rows = N_EXPERT * CAP
    source = jnp.arange(N_EXPERT, dtype=jnp.int32)[:, None]
    dest = (per_src * total_rows + source * CAP + slot).reshape(-1).astype(jnp.int32)
    token_of = (jnp.arange(TOKENS * TOPK, dtype=jnp.int32) // TOPK).astype(jnp.int32)
    table = jnp.full((EXPERTS * total_rows,), TOKENS, jnp.int32).at[dest].set(token_of)
    padded = jnp.concatenate([tokens, jnp.zeros((1, D), jnp.bfloat16)], axis=0)
    table = table.reshape(EXPERTS, total_rows)
    block = FF // N_PIPE

    def one_expert(index):
        rows = jnp.take(padded, table[index], axis=0)
        rf = rows.astype(jnp.float32)
        scale = lax.rsqrt(lax.optimization_barrier(jnp.mean(rf * rf, axis=1)) + eps)[:, None]
        gate = scale * jnp.dot(rows, w_gate[index], preferred_element_type=jnp.float32)
        up = scale * jnp.dot(rows, w_up[index], preferred_element_type=jnp.float32)
        hidden = (jax.nn.silu(gate) * up).astype(jnp.bfloat16)
        hb = hidden.reshape(total_rows, N_PIPE, block).astype(jnp.float32)
        wd = w_down[index].reshape(N_PIPE, block, D).astype(jnp.float32)
        parts = jnp.einsum('rbf,bfd->brd', hb, wd).astype(jnp.bfloat16)
        parts = lax.optimization_barrier(parts)
        return lax.optimization_barrier(jnp.sum(parts.astype(jnp.float32), axis=0)).astype(jnp.bfloat16)
    outputs = lax.map(one_expert, jnp.arange(EXPERTS, dtype=jnp.int32))
    flat_out = outputs.reshape(EXPERTS * total_rows, D)
    picked = jnp.take(flat_out, dest, axis=0).reshape(TOKENS, TOPK, D).astype(jnp.float32)
    mixed = lax.optimization_barrier(jnp.sum(weight[:, :, None] * picked, axis=1))
    return mixed.astype(jnp.bfloat16)
```

```python
import functools

import jax
import jax.numpy as jnp
from jax import lax
from jax.experimental import pallas as pl
from jax.experimental.pallas import tpu as pltpu
from jax.sharding import PartitionSpec as P

eps = 1e-06
MESH = pl.DeviceIdType.MESH
BF = jnp.bfloat16
F32 = jnp.float32
SLOT = 8


def dot(a, b, ca=1, cb=0):
    return lax.dot_general(a, b, (((ca,), (cb,)), ((), ())), preferred_element_type=F32)


def iota(shape, axis):
    return lax.broadcasted_iota(jnp.int32, shape, axis)


def kernel(
    cfg,
    tok_hbm,
    routes_hbm,
    router_hbm,
    wg_hbm,
    wu_hbm,
    wd_hbm,
    out_ref,
    tokx,
    routes,
    router,
    wgx,
    wd_raw,
    wd_stage,
    wd_pair,
    place,
    outgoing,
    incoming,
    xg,
    acc,
    acc_ss,
    hid2,
    hid_own,
    rst,
    rsr,
    ret_out,
    ret_in,
    lg_send,
    lg_recv,
    load_sem,
    wload_sem,
    disp_send,
    disp_recv,
    disp_own,
    lg_ssem,
    lg_rsem,
    wd_sem,
    ag_ssem,
    ag_rsem,
    sib_ssem,
    sib_rsem,
    hid_ssem,
    hid_rsem,
    rs_ssem,
    rs_rsem,
    ret_send,
    ret_recv,
    ret_own,
):
    n_pipe, n_exp, nx, tok, topk, cap, pw, width = cfg
    ny = n_pipe // 2
    far = ny // 2
    nz = n_exp // nx
    lanes = xg.shape[2]
    fb = wd_raw.shape[0]
    rows = n_exp * cap
    half = rows // 2
    slots = n_exp * SLOT
    hslots = slots // 2
    me_p = lax.axis_index("pipe")
    me_e = lax.axis_index("expert")
    y = me_p // 2
    c = me_p % 2
    ez = me_e // nx
    ex = me_e % nx

    def peer_of(i):
        return ((ez + i // nx) % nz) * nx + (ex + i % nx) % nx

    def pipe_dev(rel):
        return {"pipe": 2 * ((y + rel + ny) % ny) + c}

    sib = {"pipe": 2 * y + 1 - c}

    load_tok = pltpu.make_async_copy(tok_hbm, tokx.at[pl.ds(0, pw)], load_sem.at[0])
    load_routes = pltpu.make_async_copy(routes_hbm, routes, load_sem.at[1])
    load_router = pltpu.make_async_copy(router_hbm, router, load_sem.at[2])
    load_wd = pltpu.make_async_copy(wd_hbm.at[0], wd_raw, load_sem.at[3])
    load_tok.start()
    load_routes.start()
    load_router.start()
    load_wd.start()

    barrier = pltpu.get_barrier_semaphore()

    def greet_expert(i, _):
        pl.semaphore_signal(barrier, inc=1, device_id={"expert": peer_of(i)}, device_id_type=MESH)
        return 0

    def greet_pipe(i, _):
        pl.semaphore_signal(
            barrier, inc=1, device_id={"pipe": (me_p + i) % n_pipe}, device_id_type=MESH
        )
        return 0

    lax.fori_loop(1, n_exp, greet_expert, 0)
    lax.fori_loop(1, n_pipe, greet_pipe, 0)

    def load_w(p, _):
        src = pl.ds(pl.multiple_of(p * pw, 16), pw)
        pltpu.make_async_copy(
            wg_hbm.at[0, src], wgx.at[p, pl.ds(0, pw), pl.ds(0, fb)], wload_sem.at[0]
        ).start()
        pltpu.make_async_copy(
            wu_hbm.at[0, src], wgx.at[p, pl.ds(0, pw), pl.ds(fb, fb)], wload_sem.at[1]
        ).start()
        return 0

    lax.fori_loop(0, n_pipe, load_w, 0)

    load_routes.wait()
    expert_of = iota((slots, tok), 0) // SLOT
    slot_of = (iota((slots, tok), 0) % SLOT).astype(F32)
    named = jnp.where(routes[0:1, :] == expert_of, 1.0, 0.0)
    for k in range(1, topk):
        named = named + jnp.where(routes[k : k + 1, :] == expert_of, 1.0, 0.0)
    earlier = jnp.where(iota((tok, tok), 0) < iota((tok, tok), 1), 1.0, 0.0).astype(BF)
    count = dot(named.astype(BF), earlier)
    placed = jnp.where(count == slot_of, named, 0.0)
    place[...] = placed

    load_tok.wait()
    tf = tokx[0:pw, :].astype(F32)
    square = jnp.sum(tf * tf, axis=0, keepdims=True)
    hi = square.astype(BF).astype(F32)
    mid = (square - hi).astype(BF).astype(F32)
    lo = square - hi - mid
    spare = iota((lanes - pw, tok), 0)
    tokx[pw:lanes, :] = jnp.where(
        spare == 0, hi, jnp.where(spare == 1, mid, jnp.where(spare == 2, lo, 0.0))
    ).astype(BF)
    outgoing[...] = (
        dot(placed.astype(BF), tokx[...], 1, 1).astype(BF).reshape(n_exp, SLOT, lanes)
    )

    pl.semaphore_wait(barrier, n_exp - 1 + n_pipe - 1)

    def dispatch(i, _):
        dest = peer_of(i)
        pltpu.make_async_remote_copy(
            src_ref=outgoing.at[dest],
            dst_ref=incoming.at[me_e],
            send_sem=disp_send,
            recv_sem=disp_recv,
            device_id={"expert": dest},
            device_id_type=MESH,
        ).start()
        return 0

    lax.fori_loop(1, n_exp, dispatch, 0)
    own_block = pltpu.make_async_copy(outgoing.at[me_e], incoming.at[me_e], disp_own)
    own_block.start()

    load_router.wait()
    part = dot(router[...], tokx[0:pw, :])
    picks = []
    for k in range(topk):
        picks.append(
            jnp.sum(
                jnp.where(iota((n_exp, tok), 0) == routes[k : k + 1, :], part, 0.0),
                axis=0,
                keepdims=True,
            )
        )
    row8 = iota((8, tok), 0)
    packed = jnp.where(row8 == topk, square, 0.0)
    for k in range(topk):
        packed = jnp.where(row8 == k, picks[k], packed)
    lg_send[...] = packed
    lg_recv[pl.ds(me_p, 1)] = packed[None]

    def send_logits(i, _):
        pltpu.make_async_remote_copy(
            src_ref=lg_send,
            dst_ref=lg_recv.at[me_p],
            send_sem=lg_ssem,
            recv_sem=lg_rsem,
            device_id={"pipe": (me_p + i) % n_pipe},
            device_id_type=MESH,
        ).start()
        return 0

    lax.fori_loop(1, n_pipe, send_logits, 0)

    load_wd.wait()
    for p in range(n_pipe):
        base = (pw * p) // 128 * 128
        off = pw * p - base
        span = min(-(-(off + pw) // 128) * 128, wd_raw.shape[1] - base)
        shift = (iota((span, lanes), 0) == iota((span, lanes), 1) + off) & (
            iota((span, lanes), 1) < pw
        )
        wd_stage[p % 2, p // 2] = dot(
            wd_raw[:, base : base + span], jnp.where(shift, 1.0, 0.0).astype(BF)
        ).astype(BF)
    wd_own = pltpu.make_async_copy(wd_stage.at[c], wd_pair.at[:, pl.ds(0, fb)], wd_sem.at[0])
    wd_own.start()
    wd_sib = pltpu.make_async_remote_copy(
        src_ref=wd_stage.at[1 - c],
        dst_ref=wd_pair.at[:, pl.ds(fb, fb)],
        send_sem=wd_sem.at[1],
        recv_sem=wd_sem.at[2],
        device_id=sib,
        device_id_type=MESH,
    )
    wd_sib.start()
    wgx[:, pw:lanes, :] = jnp.zeros((n_pipe, lanes - pw, 2 * fb), BF)
    for j in range(2):
        everything = wgx.at[:, pl.ds(0, pw), pl.ds(j * fb, fb)]
        pltpu.make_async_copy(everything, everything, wload_sem.at[j]).wait()

    slot_id = iota((half, hslots), 1)
    target = (slot_id // SLOT) * cap + slot_id % SLOT
    pick = jnp.where(
        (iota((half, hslots), 0) == target) & (slot_id % SLOT < cap), 1.0, 0.0
    ).astype(BF)
    own_block.wait()
    arrived = incoming.at[pl.ds(0, n_exp - 1)]
    pltpu.make_async_copy(arrived, arrived, disp_recv).wait()

    def block_of(rel):
        return 2 * ((y + rel + ny) % ny) + c

    def block_sib(rel):
        return 2 * ((y + rel + ny) % ny) + 1 - c

    def part_of(p, h):
        return xg.at[p, pl.ds(h * half, half)]

    def forward(way, d, h):
        sign = 1 if way == 0 else -1
        p = block_of(-sign * d)
        return pltpu.make_async_remote_copy(
            src_ref=part_of(p, h),
            dst_ref=part_of(p, h),
            send_sem=ag_ssem.at[way, d, h],
            recv_sem=ag_rsem.at[way, d, h],
            device_id=pipe_dev(sign),
            device_id_type=MESH,
        )

    def arrival(way, d, h):
        sign = 1 if way == 0 else -1
        p = block_of(-sign * d)
        return pltpu.make_async_remote_copy(
            src_ref=part_of(p, h),
            dst_ref=part_of(p, h),
            send_sem=ag_ssem.at[way, d - 1, h],
            recv_sem=ag_rsem.at[way, d - 1, h],
            device_id=pipe_dev(sign),
            device_id_type=MESH,
        )

    def to_sibling(rel, h):
        p = block_of(rel)
        return pltpu.make_async_remote_copy(
            src_ref=part_of(p, h),
            dst_ref=part_of(p, h),
            send_sem=sib_ssem.at[rel % ny, h],
            recv_sem=sib_rsem.at[rel % ny, h],
            device_id=sib,
            device_id_type=MESH,
        )

    def from_sibling(rel, h):
        p = block_sib(rel)
        return pltpu.make_async_remote_copy(
            src_ref=part_of(p, h),
            dst_ref=part_of(p, h),
            send_sem=sib_ssem.at[rel % ny, h],
            recv_sem=sib_rsem.at[rel % ny, h],
            device_id=sib,
            device_id_type=MESH,
        )

    def travels(way, d, h):
        return d < far - 1 or (d == far - 1 and h == way)

    sent = []

    def go(copy):
        copy.start()
        sent.append(copy)

    def gather_math(blocks, first=False):
        total = None
        total_ss = None
        for p in blocks:
            one = dot(xg[p], wgx[p])
            ss = xg[p, :, lanes - 128 : lanes].astype(F32)
            total = one if total is None else total + one
            total_ss = ss if total_ss is None else total_ss + ss
        if first:
            acc[...] = total
            acc_ss[...] = total_ss
        else:
            acc[...] += total
            acc_ss[...] += total_ss

    me_block = block_of(0)
    for h in range(2):
        flat = incoming[h * (n_exp // 2) : (h + 1) * (n_exp // 2)].reshape(hslots, lanes)
        xg[me_block, h * half : (h + 1) * half, :] = dot(pick, flat).astype(BF)
        for way in range(2):
            if travels(way, 0, h):
                go(forward(way, 0, h))
        go(to_sibling(0, h))
    gather_math([me_block], first=True)
    for d in range(1, far):
        for h in range(2):
            for way in range(2):
                rel = -d if way == 0 else d
                arrival(way, d, h).wait_recv()
                if travels(way, d, h):
                    go(forward(way, d, h))
                go(to_sibling(rel, h))
        behind = [0] if d == 1 else [-(d - 1), d - 1]
        for rel in behind:
            for h in range(2):
                from_sibling(rel, h).wait_recv()
        gather_math(
            [block_sib(rel) for rel in behind] + [block_of(-d), block_of(d)]
        )
    for h in range(2):
        arrival(h, far, h).wait_recv()
        go(to_sibling(far, h))
    behind = [-(far - 1), far - 1] if far > 1 else [0]
    for rel in behind:
        for h in range(2):
            from_sibling(rel, h).wait_recv()
    gather_math([block_sib(rel) for rel in behind] + [block_of(far)])
    for h in range(2):
        from_sibling(far, h).wait_recv()
    gather_math([block_sib(far)])

    first_spare = pw - (lanes - 128)
    hid_copies = []
    for h in range(2):
        r = slice(h * half, (h + 1) * half)
        ss_lane = iota((half, 128), 1)
        ss = jnp.where((ss_lane >= first_spare) & (ss_lane < first_spare + 3), acc_ss[r, :], 0.0)
        scale = lax.rsqrt(jnp.sum(ss, axis=1, keepdims=True) / width + eps)
        gate = scale * acc[r, 0:fb]
        up = scale * acc[r, fb : 2 * fb]
        hidden = ((gate / (1.0 + jnp.exp(-gate))) * up).astype(BF)
        hid2[r, 0:fb] = hidden
        hid_own[r, :] = hidden
        copy = pltpu.make_async_remote_copy(
            src_ref=hid_own.at[pl.ds(h * half, half)],
            dst_ref=hid2.at[pl.ds(h * half, half), pl.ds(fb, fb)],
            send_sem=hid_ssem.at[h],
            recv_sem=hid_rsem.at[h],
            device_id=sib,
            device_id_type=MESH,
        )
        copy.start()
        hid_copies.append(copy)
    wd_own.wait()
    wd_sib.wait()
    for copy in hid_copies:
        copy.wait()

    def contribution(rel, h):
        return dot(hid2[h * half : (h + 1) * half, :], wd_pair[(y + rel + ny) % ny])

    def pass_on(way, s, h):
        sign = 1 if way == 0 else -1
        return pltpu.make_async_remote_copy(
            src_ref=rst.at[way, s, h],
            dst_ref=rsr.at[way, s, h],
            send_sem=rs_ssem.at[way, s, h],
            recv_sem=rs_rsem.at[way, s, h],
            device_id=pipe_dev(sign),
            device_id_type=MESH,
        )

    for s in range(far):
        for turn in range(2):
            for way in range(2):
                h = 1 - way if turn == 0 else way
                if s == 0 and h != way:
                    continue
                rel = (far - s) * (1 if way == 0 else -1)
                total = contribution(rel, h)
                if s > 1 or (s == 1 and h == way):
                    pass_on(way, s - 1, h).wait_recv()
                    total = total + rsr[way, s - 1, h].astype(F32)
                rst[way, s, h] = total.astype(BF)
                go(pass_on(way, s, h))

    spread = (iota((hslots, half), 0) // SLOT) * cap + iota((hslots, half), 0) % SLOT
    unpick = jnp.where(
        (iota((hslots, half), 1) == spread) & (iota((hslots, half), 0) % SLOT < cap), 1.0, 0.0
    ).astype(BF)
    for h in range(2):
        total = contribution(0, h)
        for way in range(2):
            if far > 1 or h == way:
                pass_on(way, far - 1, h).wait_recv()
                total = total + rsr[way, far - 1, h].astype(F32)
        ret_out[h * (n_exp // 2) : (h + 1) * (n_exp // 2)] = (
            dot(unpick, total.astype(BF)).astype(BF).reshape(n_exp // 2, SLOT, lanes)
        )

    def give_back(i, _):
        dest = peer_of(i)
        pltpu.make_async_remote_copy(
            src_ref=ret_out.at[dest],
            dst_ref=ret_in.at[me_e],
            send_sem=ret_send,
            recv_sem=ret_recv,
            device_id={"expert": dest},
            device_id_type=MESH,
        ).start()
        return 0

    lax.fori_loop(1, n_exp, give_back, 0)
    own_back = pltpu.make_async_copy(ret_out.at[me_e], ret_in.at[me_e], ret_own)
    own_back.start()

    others = lg_recv.at[pl.ds(0, n_pipe - 1)]
    pltpu.make_async_copy(others, others, lg_rsem).wait()
    sums = jnp.sum(lg_recv[...], axis=0)
    rstd = lax.rsqrt(sums[topk : topk + 1, :] / width + eps)
    scores = []
    for k in range(topk):
        logit = rstd * sums[k : k + 1, :]
        small = jnp.exp(-jnp.abs(logit))
        scores.append(jnp.where(logit >= 0, 1.0, small) / (1.0 + small))
    norm = scores[0]
    for k in range(1, topk):
        norm = norm + scores[k]
    weighted = jnp.zeros((slots, tok), F32)
    for k in range(topk):
        weighted = jnp.where(routes[k : k + 1, :] == expert_of, scores[k] / norm, weighted)
    weighted = weighted * place[...]
    w_hi = weighted.astype(BF)
    w_lo = (weighted - w_hi.astype(F32)).astype(BF)

    for copy in sent:
        copy.wait_send()
    block63 = outgoing.at[pl.ds(0, n_exp - 1)]
    pltpu.make_async_copy(block63, block63, disp_send).wait()
    sent15 = lg_recv.at[pl.ds(0, n_pipe - 1)]
    pltpu.make_async_copy(sent15, sent15, lg_ssem).wait()

    own_back.wait()
    back63 = ret_in.at[pl.ds(0, n_exp - 1)]
    pltpu.make_async_copy(back63, back63, ret_recv).wait()
    got = ret_in[...].reshape(slots, lanes)
    mixed = dot(got, w_hi, 0, 0) + dot(got, w_lo, 0, 0)
    out_ref[...] = mixed[0:pw, :].astype(BF)
    left63 = ret_out.at[pl.ds(0, n_exp - 1)]
    pltpu.make_async_copy(left63, left63, ret_send).wait()


def body(tokens, routes, router, w_gate, w_up, w_down):
    tok, pw = tokens.shape
    topk = routes.shape[1]
    n_exp = lax.axis_size("expert")
    n_pipe = lax.axis_size("pipe")
    cap = max(2, tok * topk // n_exp + max(1, tok * topk // (4 * n_exp)))
    width = pw * n_pipe
    lanes = -(-(pw + 3) // 128) * 128
    fb = w_gate.shape[2]
    ny = n_pipe // 2
    far = ny // 2
    rows = n_exp * cap
    half = rows // 2
    nx = 8 if n_exp % 8 == 0 else n_exp
    cfg = (n_pipe, n_exp, nx, tok, topk, cap, pw, width)
    dma = pltpu.SemaphoreType.DMA
    scratch = [
        pltpu.VMEM((lanes, tok), BF),
        pltpu.VMEM((topk, tok), jnp.int32),
        pltpu.VMEM((n_exp, pw), BF),
        pltpu.VMEM((n_pipe, lanes, 2 * fb), BF),
        pltpu.VMEM((fb, width), BF),
        pltpu.VMEM((2, ny, fb, lanes), BF),
        pltpu.VMEM((ny, 2 * fb, lanes), BF),
        pltpu.VMEM((n_exp * SLOT, tok), F32),
        pltpu.VMEM((n_exp, SLOT, lanes), BF),
        pltpu.VMEM((n_exp, SLOT, lanes), BF),
        pltpu.VMEM((n_pipe, rows, lanes), BF),
        pltpu.VMEM((rows, 2 * fb), F32),
        pltpu.VMEM((rows, 128), F32),
        pltpu.VMEM((rows, 2 * fb), BF),
        pltpu.VMEM((rows, fb), BF),
        pltpu.VMEM((2, far, 2, half, lanes), BF),
        pltpu.VMEM((2, far, 2, half, lanes), BF),
        pltpu.VMEM((n_exp, SLOT, lanes), BF),
        pltpu.VMEM((n_exp, SLOT, lanes), BF),
        pltpu.VMEM((8, tok), F32),
        pltpu.VMEM((n_pipe, 8, tok), F32),
        dma((4,)),
        dma((2,)),
        dma,
        dma,
        dma,
        dma,
        dma,
        dma((3,)),
        dma((2, far, 2)),
        dma((2, far, 2)),
        dma((ny, 2)),
        dma((ny, 2)),
        dma((2,)),
        dma((2,)),
        dma((2, far, 2)),
        dma((2, far, 2)),
        dma,
        dma,
        dma,
    ]
    mixed = pl.pallas_call(
        functools.partial(kernel, cfg),
        out_shape=jax.ShapeDtypeStruct((pw, tok), BF),
        in_specs=[pl.BlockSpec(memory_space=pl.ANY)] * 6,
        out_specs=pl.BlockSpec(memory_space=pltpu.VMEM),
        scratch_shapes=scratch,
        compiler_params=pltpu.CompilerParams(
            collective_id=0, has_side_effects=True, vmem_limit_bytes=40 << 20
        ),
    )(tokens.T, routes.T, router.T, w_gate, w_up, w_down)
    return mixed.T


def solution(mesh):
    placed = (
        P("expert", "pipe"),
        P("expert", None),
        P("pipe", None),
        P("expert", None, "pipe"),
        P("expert", None, "pipe"),
        P("expert", "pipe", None),
    )
    return jax.shard_map(
        body, mesh=mesh, in_specs=placed, out_specs=P("expert", "pipe"), check_vma=False
    )
```

```python
import functools

import jax
import jax.numpy as jnp
from jax import lax
from jax.experimental import pallas as pl
from jax.experimental.pallas import tpu as pltpu
from jax.sharding import PartitionSpec as P

eps = 1e-06
MESH = pl.DeviceIdType.MESH
BF = jnp.bfloat16
F32 = jnp.float32
SLOT = 8


def dot(a, b, ca=1, cb=0):
    return lax.dot_general(a, b, (((ca,), (cb,)), ((), ())), preferred_element_type=F32)


def iota(shape, axis):
    return lax.broadcasted_iota(jnp.int32, shape, axis)


def kernel(
    cfg,
    tok_hbm,
    routes_hbm,
    router_hbm,
    wg_hbm,
    wu_hbm,
    wd_hbm,
    out_ref,
    tokx,
    routes,
    router,
    wgx,
    wd_raw,
    wd_stage,
    wd_pair,
    place,
    outgoing,
    incoming,
    xg,
    acc,
    acc_ss,
    hid2,
    hid_own,
    rst,
    rsr,
    ret_out,
    ret_in,
    lg_send,
    lg_recv,
    load_sem,
    wload_sem,
    disp_send,
    disp_recv,
    disp_own,
    lg_ssem,
    lg_rsem,
    wd_sem,
    ag_ssem,
    ag_rsem,
    sib_ssem,
    sib_rsem,
    hid_ssem,
    hid_rsem,
    rs_ssem,
    rs_rsem,
    ret_send,
    ret_recv,
    ret_own,
):
    n_pipe, n_exp, nx, tok, topk, cap, pw, width, turns = cfg
    ny = n_pipe // 2
    far = ny // 2
    nz = n_exp // nx
    lanes = xg.shape[2]
    fb = wd_raw.shape[0]
    rows = n_exp * cap
    half = rows // turns
    slots = n_exp * SLOT
    hslots = slots // turns
    group = n_exp // turns
    me_p = lax.axis_index("pipe")
    me_e = lax.axis_index("expert")
    y = me_p // 2
    c = me_p % 2
    ez = me_e // nx
    ex = me_e % nx

    def offset(i):
        if nz < 4:
            return 0, i % nx
        row, col = nz - 1 - i // nx, i % nx
        dz = jnp.where(row % 2 == 1, (row + 1) // 2, nz - (row + 1) // 2)
        return dz, col + nx // 2

    self_step = 0 if nz < 4 else (nz - 1) * nx + nx // 2
    self_turn = self_step // group

    def peer_of(i):
        dz, dx = offset(i)
        return ((ez + dz) % nz) * nx + (ex + dx) % nx

    def source_of(i):
        dz, dx = offset(i)
        return ((ez + 2 * nz - dz) % nz) * nx + (ex + 2 * nx - dx) % nx

    def each_step(low, high, do):
        if low <= self_step < high:
            lax.fori_loop(low, self_step, do, 0)
            lax.fori_loop(self_step + 1, high, do, 0)
        else:
            lax.fori_loop(low, high, do, 0)

    def pipe_dev(rel):
        return {"pipe": 2 * ((y + rel + ny) % ny) + c}

    sib = {"pipe": 2 * y + 1 - c}

    load_tok = pltpu.make_async_copy(tok_hbm, tokx.at[pl.ds(0, pw)], load_sem.at[0])
    load_routes = pltpu.make_async_copy(routes_hbm, routes, load_sem.at[1])
    load_router = pltpu.make_async_copy(router_hbm, router, load_sem.at[2])
    load_wd = pltpu.make_async_copy(wd_hbm.at[0], wd_raw, load_sem.at[3])
    load_tok.start()
    load_routes.start()
    load_router.start()
    load_wd.start()

    barrier = pltpu.get_barrier_semaphore()

    def greet_expert(i, _):
        pl.semaphore_signal(barrier, inc=1, device_id={"expert": peer_of(i)}, device_id_type=MESH)
        return 0

    def greet_pipe(i, _):
        pl.semaphore_signal(
            barrier, inc=1, device_id={"pipe": (me_p + i) % n_pipe}, device_id_type=MESH
        )
        return 0

    each_step(0, n_exp, greet_expert)
    lax.fori_loop(1, n_pipe, greet_pipe, 0)

    def load_w(p, _):
        src = pl.ds(pl.multiple_of(p * pw, 16), pw)
        pltpu.make_async_copy(
            wg_hbm.at[0, src], wgx.at[p, pl.ds(0, pw), pl.ds(0, fb)], wload_sem.at[0]
        ).start()
        pltpu.make_async_copy(
            wu_hbm.at[0, src], wgx.at[p, pl.ds(0, pw), pl.ds(fb, fb)], wload_sem.at[1]
        ).start()
        return 0

    lax.fori_loop(0, n_pipe, load_w, 0)

    load_routes.wait()
    expert_of = iota((slots, tok), 0) // SLOT
    slot_of = (iota((slots, tok), 0) % SLOT).astype(F32)
    named = jnp.where(routes[0:1, :] == expert_of, 1.0, 0.0)
    for k in range(1, topk):
        named = named + jnp.where(routes[k : k + 1, :] == expert_of, 1.0, 0.0)
    earlier = jnp.where(iota((tok, tok), 0) < iota((tok, tok), 1), 1.0, 0.0).astype(BF)
    count = dot(named.astype(BF), earlier)
    placed = jnp.where(count == slot_of, named, 0.0)
    place[...] = placed

    load_tok.wait()
    tf = tokx[0:pw, :].astype(F32)
    square = jnp.sum(tf * tf, axis=0, keepdims=True)
    hi = square.astype(BF).astype(F32)
    mid = (square - hi).astype(BF).astype(F32)
    lo = square - hi - mid
    spare = iota((lanes - pw, tok), 0)
    tokx[pw:lanes, :] = jnp.where(
        spare == 0, hi, jnp.where(spare == 1, mid, jnp.where(spare == 2, lo, 0.0))
    ).astype(BF)
    outgoing[...] = (
        dot(placed.astype(BF), tokx[...], 1, 1).astype(BF).reshape(n_exp, SLOT, lanes)
    )

    pl.semaphore_wait(barrier, n_exp - 1 + n_pipe - 1)

    def dispatch(i, _):
        dest = peer_of(i)
        pltpu.make_async_remote_copy(
            src_ref=outgoing.at[dest],
            dst_ref=incoming.at[i],
            send_sem=disp_send,
            recv_sem=disp_recv.at[i // group],
            device_id={"expert": dest},
            device_id_type=MESH,
        ).start()
        return 0

    own_block = pltpu.make_async_copy(outgoing.at[me_e], incoming.at[self_step], disp_own)
    own_block.start()
    each_step(0, n_exp, dispatch)

    load_router.wait()
    part = dot(router[...], tokx[0:pw, :])
    picks = []
    for k in range(topk):
        picks.append(
            jnp.sum(
                jnp.where(iota((n_exp, tok), 0) == routes[k : k + 1, :], part, 0.0),
                axis=0,
                keepdims=True,
            )
        )
    row8 = iota((8, tok), 0)
    packed = jnp.where(row8 == topk, square, 0.0)
    for k in range(topk):
        packed = jnp.where(row8 == k, picks[k], packed)
    lg_send[...] = packed
    lg_recv[pl.ds(me_p, 1)] = packed[None]

    def send_logits(i, _):
        pltpu.make_async_remote_copy(
            src_ref=lg_send,
            dst_ref=lg_recv.at[me_p],
            send_sem=lg_ssem,
            recv_sem=lg_rsem,
            device_id={"pipe": (me_p + i) % n_pipe},
            device_id_type=MESH,
        ).start()
        return 0

    lax.fori_loop(1, n_pipe, send_logits, 0)

    load_wd.wait()
    for p in range(n_pipe):
        base = (pw * p) // 128 * 128
        off = pw * p - base
        span = min(-(-(off + pw) // 128) * 128, wd_raw.shape[1] - base)
        shift = (iota((span, lanes), 0) == iota((span, lanes), 1) + off) & (
            iota((span, lanes), 1) < pw
        )
        wd_stage[p % 2, p // 2] = dot(
            wd_raw[:, base : base + span], jnp.where(shift, 1.0, 0.0).astype(BF)
        ).astype(BF)
    wd_own = pltpu.make_async_copy(wd_stage.at[c], wd_pair.at[:, pl.ds(0, fb)], wd_sem.at[0])
    wd_own.start()
    wd_sib = pltpu.make_async_remote_copy(
        src_ref=wd_stage.at[1 - c],
        dst_ref=wd_pair.at[:, pl.ds(fb, fb)],
        send_sem=wd_sem.at[1],
        recv_sem=wd_sem.at[2],
        device_id=sib,
        device_id_type=MESH,
    )
    wd_sib.start()
    wgx[:, pw:lanes, :] = jnp.zeros((n_pipe, lanes - pw, 2 * fb), BF)
    for j in range(2):
        everything = wgx.at[:, pl.ds(0, pw), pl.ds(j * fb, fb)]
        pltpu.make_async_copy(everything, everything, wload_sem.at[j]).wait()

    slot_id = iota((half, hslots), 1)
    target = (slot_id // SLOT) * cap + slot_id % SLOT
    pick = jnp.where(
        (iota((half, hslots), 0) == target) & (slot_id % SLOT < cap), 1.0, 0.0
    ).astype(BF)

    def block_of(rel):
        return 2 * ((y + rel + ny) % ny) + c

    def block_sib(rel):
        return 2 * ((y + rel + ny) % ny) + 1 - c

    def part_of(p, h):
        return xg.at[p, pl.ds(h * half, half)]

    def forward(way, d, h):
        sign = 1 if way == 0 else -1
        p = block_of(-sign * d)
        return pltpu.make_async_remote_copy(
            src_ref=part_of(p, h),
            dst_ref=part_of(p, h),
            send_sem=ag_ssem.at[way, d, h],
            recv_sem=ag_rsem.at[way, d, h],
            device_id=pipe_dev(sign),
            device_id_type=MESH,
        )

    def arrival(way, d, h):
        sign = 1 if way == 0 else -1
        p = block_of(-sign * d)
        return pltpu.make_async_remote_copy(
            src_ref=part_of(p, h),
            dst_ref=part_of(p, h),
            send_sem=ag_ssem.at[way, d - 1, h],
            recv_sem=ag_rsem.at[way, d - 1, h],
            device_id=pipe_dev(sign),
            device_id_type=MESH,
        )

    def to_sibling(rel, h):
        p = block_of(rel)
        return pltpu.make_async_remote_copy(
            src_ref=part_of(p, h),
            dst_ref=part_of(p, h),
            send_sem=sib_ssem.at[rel % ny, h],
            recv_sem=sib_rsem.at[rel % ny, h],
            device_id=sib,
            device_id_type=MESH,
        )

    def from_sibling(rel, h):
        p = block_sib(rel)
        return pltpu.make_async_remote_copy(
            src_ref=part_of(p, h),
            dst_ref=part_of(p, h),
            send_sem=sib_ssem.at[rel % ny, h],
            recv_sem=sib_rsem.at[rel % ny, h],
            device_id=sib,
            device_id_type=MESH,
        )

    def travels(way, d, h):
        return d < far - 1 or (d == far - 1 and h % 2 == way)

    sent = []

    def go(copy):
        copy.start()
        sent.append(copy)

    def gather_math(blocks, h, first=False):
        r = slice(h * half, (h + 1) * half)
        total = None
        total_ss = None
        for p in blocks:
            one = dot(xg[p, r, :], wgx[p])
            ss = xg[p, r, lanes - 128 : lanes].astype(F32)
            total = one if total is None else total + one
            total_ss = ss if total_ss is None else total_ss + ss
        if first:
            acc[r, :] = total
            acc_ss[r, :] = total_ss
        else:
            acc[r, :] += total
            acc_ss[r, :] += total_ss

    def start_gather(h):
        here = group - 1 if h == self_turn else group
        if h == self_turn:
            own_block.wait()
        if here > 0:
            arrived = incoming.at[pl.ds(0, here)]
            pltpu.make_async_copy(arrived, arrived, disp_recv.at[h]).wait()
        flat = incoming[h * group : (h + 1) * group].reshape(hslots, lanes)
        me_block = block_of(0)
        xg[me_block, h * half : (h + 1) * half, :] = dot(pick, flat).astype(BF)
        for way in range(2):
            if travels(way, 0, h):
                go(forward(way, 0, h))
        go(to_sibling(0, h))
        gather_math([me_block], h, first=True)

    def step_gather(d, h):
        for way in range(2):
            rel = -d if way == 0 else d
            arrival(way, d, h).wait_recv()
            if travels(way, d, h):
                go(forward(way, d, h))
            go(to_sibling(rel, h))
        behind = [0] if d == 1 else [-(d - 1), d - 1]
        for rel in behind:
            from_sibling(rel, h).wait_recv()
        gather_math([block_sib(rel) for rel in behind] + [block_of(-d), block_of(d)], h)

    def end_gather(h):
        arrival(h % 2, far, h).wait_recv()
        go(to_sibling(far, h))
        behind = [-(far - 1), far - 1] if far > 1 else [0]
        for rel in behind:
            from_sibling(rel, h).wait_recv()
        gather_math([block_sib(rel) for rel in behind] + [block_of(far)], h)
        from_sibling(far, h).wait_recv()
        gather_math([block_sib(far)], h)

    first_spare = pw - (lanes - 128)

    def share_hidden(h):
        r = slice(h * half, (h + 1) * half)
        ss_lane = iota((half, 128), 1)
        ss = jnp.where((ss_lane >= first_spare) & (ss_lane < first_spare + 3), acc_ss[r, :], 0.0)
        scale = lax.rsqrt(jnp.sum(ss, axis=1, keepdims=True) / width + eps)
        gate = scale * acc[r, 0:fb]
        up = scale * acc[r, fb : 2 * fb]
        hidden = ((gate / (1.0 + jnp.exp(-gate))) * up).astype(BF)
        hid2[r, 0:fb] = hidden
        hid_own[r, :] = hidden
        copy = pltpu.make_async_remote_copy(
            src_ref=hid_own.at[pl.ds(h * half, half)],
            dst_ref=hid2.at[pl.ds(h * half, half), pl.ds(fb, fb)],
            send_sem=hid_ssem.at[h],
            recv_sem=hid_rsem.at[h],
            device_id=sib,
            device_id_type=MESH,
        )
        go(copy)
        return copy

    def contribution(rel, h):
        return dot(hid2[h * half : (h + 1) * half, :], wd_pair[(y + rel + ny) % ny])

    def pass_on(way, s, h):
        sign = 1 if way == 0 else -1
        return pltpu.make_async_remote_copy(
            src_ref=rst.at[way, s, h],
            dst_ref=rsr.at[way, s, h],
            send_sem=rs_ssem.at[way, s, h],
            recv_sem=rs_rsem.at[way, s, h],
            device_id=pipe_dev(sign),
            device_id_type=MESH,
        )

    def add_and_pass(way, s, h, adds):
        total = contribution((far - s) * (1 if way == 0 else -1), h)
        if adds:
            pass_on(way, s - 1, h).wait_recv()
            total = total + rsr[way, s - 1, h].astype(F32)
        rst[way, s, h] = total.astype(BF)
        go(pass_on(way, s, h))

    def start_scatter(h):
        add_and_pass(h % 2, 0, h, False)
        if far > 1:
            add_and_pass(1 - h % 2, 1, h, False)

    def step_scatter(s, h):
        add_and_pass(h % 2, s, h, True)
        if s + 1 < far:
            add_and_pass(1 - h % 2, s + 1, h, True)

    spread = (iota((hslots, half), 0) // SLOT) * cap + iota((hslots, half), 0) % SLOT
    unpick = jnp.where(
        (iota((hslots, half), 1) == spread) & (iota((hslots, half), 0) % SLOT < cap), 1.0, 0.0
    ).astype(BF)

    def give_back(i, _):
        pltpu.make_async_remote_copy(
            src_ref=ret_out.at[i],
            dst_ref=ret_in.at[me_e],
            send_sem=ret_send,
            recv_sem=ret_recv,
            device_id={"expert": source_of(i)},
            device_id_type=MESH,
        ).start()
        return 0

    own_back = pltpu.make_async_copy(ret_out.at[self_step], ret_in.at[me_e], ret_own)

    def end_scatter(h):
        total = contribution(0, h)
        for way in range(2):
            if far > 1 or h % 2 == way:
                pass_on(way, far - 1, h).wait_recv()
                total = total + rsr[way, far - 1, h].astype(F32)
        ret_out[h * group : (h + 1) * group] = (
            dot(unpick, total.astype(BF)).astype(BF).reshape(group, SLOT, lanes)
        )
        each_step(h * group, (h + 1) * group, give_back)
        if h == self_turn:
            own_back.start()

    for h in range(turns):
        start_gather(h)
    for d in range(1, far):
        for h in range(turns):
            step_gather(d, h)
    wd_own.wait()
    wd_sib.wait()
    end_gather(0)
    hid_copy = share_hidden(0)
    for h in range(turns):
        if h + 1 < turns:
            end_gather(h + 1)
        hid_copy.wait_recv()
        start_scatter(h)
        if h + 1 < turns:
            hid_copy = share_hidden(h + 1)
    for t in range(1, far):
        for h in range(turns):
            step_scatter(t, h)
    for h in range(turns):
        end_scatter(h)

    others = lg_recv.at[pl.ds(0, n_pipe - 1)]
    pltpu.make_async_copy(others, others, lg_rsem).wait()
    sums = jnp.sum(lg_recv[...], axis=0)
    rstd = lax.rsqrt(sums[topk : topk + 1, :] / width + eps)
    scores = []
    for k in range(topk):
        logit = rstd * sums[k : k + 1, :]
        small = jnp.exp(-jnp.abs(logit))
        scores.append(jnp.where(logit >= 0, 1.0, small) / (1.0 + small))
    norm = scores[0]
    for k in range(1, topk):
        norm = norm + scores[k]
    weighted = jnp.zeros((slots, tok), F32)
    for k in range(topk):
        weighted = jnp.where(routes[k : k + 1, :] == expert_of, scores[k] / norm, weighted)
    weighted = weighted * place[...]
    w_hi = weighted.astype(BF)
    w_lo = (weighted - w_hi.astype(F32)).astype(BF)
    w_both = jnp.concatenate([w_hi, w_lo], axis=1)

    for copy in sent:
        copy.wait_send()
    block63 = outgoing.at[pl.ds(0, n_exp - 1)]
    pltpu.make_async_copy(block63, block63, disp_send).wait()
    sent15 = lg_recv.at[pl.ds(0, n_pipe - 1)]
    pltpu.make_async_copy(sent15, sent15, lg_ssem).wait()

    own_back.wait()
    back63 = ret_in.at[pl.ds(0, n_exp - 1)]
    pltpu.make_async_copy(back63, back63, ret_recv).wait()
    got = ret_in[...].reshape(slots, lanes)
    both = dot(got, w_both, 0, 0)
    out_ref[...] = (both[0:pw, 0:tok] + both[0:pw, tok : 2 * tok]).astype(BF)
    left63 = ret_out.at[pl.ds(0, n_exp - 1)]
    pltpu.make_async_copy(left63, left63, ret_send).wait()


def body(tokens, routes, router, w_gate, w_up, w_down):
    tok, pw = tokens.shape
    topk = routes.shape[1]
    n_exp = lax.axis_size("expert")
    n_pipe = lax.axis_size("pipe")
    cap = max(2, tok * topk // n_exp + max(1, tok * topk // (4 * n_exp)))
    width = pw * n_pipe
    lanes = -(-(pw + 3) // 128) * 128
    fb = w_gate.shape[2]
    ny = n_pipe // 2
    far = ny // 2
    rows = n_exp * cap
    nx = 8 if n_exp % 8 == 0 else n_exp
    turns = 4 if n_exp % 4 == 0 else 2
    cfg = (n_pipe, n_exp, nx, tok, topk, cap, pw, width, turns)
    dma = pltpu.SemaphoreType.DMA
    scratch = [
        pltpu.VMEM((lanes, tok), BF),
        pltpu.VMEM((topk, tok), jnp.int32),
        pltpu.VMEM((n_exp, pw), BF),
        pltpu.VMEM((n_pipe, lanes, 2 * fb), BF),
        pltpu.VMEM((fb, width), BF),
        pltpu.VMEM((2, ny, fb, lanes), BF),
        pltpu.VMEM((ny, 2 * fb, lanes), BF),
        pltpu.VMEM((n_exp * SLOT, tok), F32),
        pltpu.VMEM((n_exp, SLOT, lanes), BF),
        pltpu.VMEM((n_exp, SLOT, lanes), BF),
        pltpu.VMEM((n_pipe, rows, lanes), BF),
        pltpu.VMEM((rows, 2 * fb), F32),
        pltpu.VMEM((rows, 128), F32),
        pltpu.VMEM((rows, 2 * fb), BF),
        pltpu.VMEM((rows, fb), BF),
        pltpu.VMEM((2, far, turns, rows // turns, lanes), BF),
        pltpu.VMEM((2, far, turns, rows // turns, lanes), BF),
        pltpu.VMEM((n_exp, SLOT, lanes), BF),
        pltpu.VMEM((n_exp, SLOT, lanes), BF),
        pltpu.VMEM((8, tok), F32),
        pltpu.VMEM((n_pipe, 8, tok), F32),
        dma((4,)),
        dma((2,)),
        dma,
        dma((turns,)),
        dma,
        dma,
        dma,
        dma((3,)),
        dma((2, far, turns)),
        dma((2, far, turns)),
        dma((ny, turns)),
        dma((ny, turns)),
        dma((turns,)),
        dma((turns,)),
        dma((2, far, turns)),
        dma((2, far, turns)),
        dma,
        dma,
        dma,
    ]
    mixed = pl.pallas_call(
        functools.partial(kernel, cfg),
        out_shape=jax.ShapeDtypeStruct((pw, tok), BF),
        in_specs=[pl.BlockSpec(memory_space=pl.ANY)] * 6,
        out_specs=pl.BlockSpec(memory_space=pltpu.VMEM),
        scratch_shapes=scratch,
        compiler_params=pltpu.CompilerParams(
            collective_id=0, has_side_effects=True, vmem_limit_bytes=60 << 20
        ),
    )(tokens.T, routes.T, router.T, w_gate, w_up, w_down)
    return mixed.T


def solution(mesh):
    placed = (
        P("expert", "pipe"),
        P("expert", None),
        P("pipe", None),
        P("expert", None, "pipe"),
        P("expert", None, "pipe"),
        P("expert", "pipe", None),
    )
    return jax.shard_map(
        body, mesh=mesh, in_specs=placed, out_specs=P("expert", "pipe"), check_vma=False
    )
```

```python
import functools

import jax
import jax.numpy as jnp
from jax import lax
from jax.experimental import pallas as pl
from jax.experimental.pallas import tpu as pltpu
from jax.sharding import PartitionSpec as P

eps = 1e-06
MESH = pl.DeviceIdType.MESH
BF = jnp.bfloat16
F32 = jnp.float32
SLOT = 8


def dot(a, b, ca=1, cb=0):
    return lax.dot_general(a, b, (((ca,), (cb,)), ((), ())), preferred_element_type=F32)


def iota(shape, axis):
    return lax.broadcasted_iota(jnp.int32, shape, axis)


def kernel(
    cfg,
    tok_hbm,
    routes_hbm,
    router_hbm,
    wg_hbm,
    wu_hbm,
    wd_hbm,
    out_ref,
    tokx,
    routes,
    router,
    wgx,
    wd_raw,
    wd_stage,
    wd_pair,
    place,
    outgoing,
    incoming,
    xg,
    acc,
    acc_ss,
    hid2,
    hid_own,
    rst,
    rsr,
    ret_out,
    ret_in,
    lg_send,
    lg_recv,
    load_sem,
    wload_sem,
    disp_send,
    disp_recv,
    disp_own,
    lg_ssem,
    lg_rsem,
    wd_sem,
    ag_ssem,
    ag_rsem,
    sib_ssem,
    sib_rsem,
    hid_ssem,
    hid_rsem,
    rs_ssem,
    rs_rsem,
    ret_send,
    ret_recv,
    ret_own,
):
    n_pipe, n_exp, nx, tok, topk, cap, pw, width, turns = cfg
    ny = n_pipe // 2
    far = ny // 2
    nz = n_exp // nx
    lanes = xg.shape[2]
    fb = wd_raw.shape[0]
    rows = n_exp * cap
    half = rows // turns
    slots = n_exp * SLOT
    hslots = slots // turns
    group = n_exp // turns
    me_p = lax.axis_index("pipe")
    me_e = lax.axis_index("expert")
    y = me_p // 2
    c = me_p % 2
    ez = me_e // nx
    ex = me_e % nx

    def offset(i):
        if nz < 4:
            return 0, i % nx
        row, col = nz - 1 - i // nx, i % nx
        dz = jnp.where(row % 2 == 1, (row + 1) // 2, nz - (row + 1) // 2)
        return dz, col + nx // 2

    self_step = 0 if nz < 4 else (nz - 1) * nx + nx // 2
    self_turn = self_step // group

    def peer_of(i):
        dz, dx = offset(i)
        return ((ez + dz) % nz) * nx + (ex + dx) % nx

    def source_of(i):
        dz, dx = offset(i)
        return ((ez + 2 * nz - dz) % nz) * nx + (ex + 2 * nx - dx) % nx

    def each_step(low, high, do):
        if low <= self_step < high:
            lax.fori_loop(low, self_step, do, 0)
            lax.fori_loop(self_step + 1, high, do, 0)
        else:
            lax.fori_loop(low, high, do, 0)

    def pipe_dev(rel):
        return {"pipe": 2 * ((y + rel + ny) % ny) + c}

    sib = {"pipe": 2 * y + 1 - c}

    load_tok = pltpu.make_async_copy(tok_hbm, tokx.at[pl.ds(0, pw)], load_sem.at[0])
    load_routes = pltpu.make_async_copy(routes_hbm, routes, load_sem.at[1])
    load_router = pltpu.make_async_copy(router_hbm, router, load_sem.at[2])
    load_wd = pltpu.make_async_copy(wd_hbm.at[0], wd_raw, load_sem.at[3])
    load_tok.start()
    load_routes.start()
    load_router.start()
    load_wd.start()

    barrier = pltpu.get_barrier_semaphore()

    def greet_expert(i, _):
        pl.semaphore_signal(barrier, inc=1, device_id={"expert": peer_of(i)}, device_id_type=MESH)
        return 0

    def greet_pipe(i, _):
        pl.semaphore_signal(
            barrier, inc=1, device_id={"pipe": (me_p + i) % n_pipe}, device_id_type=MESH
        )
        return 0

    each_step(0, n_exp, greet_expert)
    lax.fori_loop(1, n_pipe, greet_pipe, 0)

    def load_w(p, _):
        src = pl.ds(pl.multiple_of(p * pw, 16), pw)
        pltpu.make_async_copy(
            wg_hbm.at[0, src], wgx.at[p, pl.ds(0, pw), pl.ds(0, fb)], wload_sem.at[0]
        ).start()
        pltpu.make_async_copy(
            wu_hbm.at[0, src], wgx.at[p, pl.ds(0, pw), pl.ds(fb, fb)], wload_sem.at[1]
        ).start()
        return 0

    lax.fori_loop(0, n_pipe, load_w, 0)

    load_routes.wait()
    expert_of = iota((slots, tok), 0) // SLOT
    slot_of = (iota((slots, tok), 0) % SLOT).astype(F32)
    named = jnp.where(routes[0:1, :] == expert_of, 1.0, 0.0)
    for k in range(1, topk):
        named = named + jnp.where(routes[k : k + 1, :] == expert_of, 1.0, 0.0)
    earlier = jnp.where(iota((tok, tok), 0) < iota((tok, tok), 1), 1.0, 0.0).astype(BF)
    count = dot(named.astype(BF), earlier)
    placed = jnp.where(count == slot_of, named, 0.0)
    place[...] = placed

    load_tok.wait()
    tf = tokx[0:pw, :].astype(F32)
    square = jnp.sum(tf * tf, axis=0, keepdims=True)
    hi = square.astype(BF).astype(F32)
    mid = (square - hi).astype(BF).astype(F32)
    lo = square - hi - mid
    spare = iota((lanes - pw, tok), 0)
    tokx[pw:lanes, :] = jnp.where(
        spare == 0, hi, jnp.where(spare == 1, mid, jnp.where(spare == 2, lo, 0.0))
    ).astype(BF)
    outgoing[...] = (
        dot(placed.astype(BF), tokx[...], 1, 1).astype(BF).reshape(n_exp, SLOT, lanes)
    )

    pl.semaphore_wait(barrier, n_exp - 1 + n_pipe - 1)

    def dispatch(i, _):
        dest = peer_of(i)
        pltpu.make_async_remote_copy(
            src_ref=outgoing.at[dest],
            dst_ref=incoming.at[i],
            send_sem=disp_send,
            recv_sem=disp_recv.at[i // group],
            device_id={"expert": dest},
            device_id_type=MESH,
        ).start()
        return 0

    own_block = pltpu.make_async_copy(outgoing.at[me_e], incoming.at[self_step], disp_own)
    own_block.start()
    each_step(0, n_exp, dispatch)

    load_router.wait()
    part = dot(router[...], tokx[0:pw, :])
    picks = []
    for k in range(topk):
        picks.append(
            jnp.sum(
                jnp.where(iota((n_exp, tok), 0) == routes[k : k + 1, :], part, 0.0),
                axis=0,
                keepdims=True,
            )
        )
    row8 = iota((8, tok), 0)
    packed = jnp.where(row8 == topk, square, 0.0)
    for k in range(topk):
        packed = jnp.where(row8 == k, picks[k], packed)
    lg_send[...] = packed
    lg_recv[pl.ds(me_p, 1)] = packed[None]

    def send_logits(i, _):
        pltpu.make_async_remote_copy(
            src_ref=lg_send,
            dst_ref=lg_recv.at[me_p],
            send_sem=lg_ssem,
            recv_sem=lg_rsem,
            device_id={"pipe": (me_p + i) % n_pipe},
            device_id_type=MESH,
        ).start()
        return 0

    lax.fori_loop(1, n_pipe, send_logits, 0)

    load_wd.wait()
    for p in range(n_pipe):
        base = (pw * p) // 128 * 128
        off = pw * p - base
        span = min(-(-(off + pw) // 128) * 128, wd_raw.shape[1] - base)
        shift = (iota((span, lanes), 0) == iota((span, lanes), 1) + off) & (
            iota((span, lanes), 1) < pw
        )
        wd_stage[p % 2, p // 2] = dot(
            wd_raw[:, base : base + span], jnp.where(shift, 1.0, 0.0).astype(BF)
        ).astype(BF)
    wd_own = pltpu.make_async_copy(wd_stage.at[c], wd_pair.at[:, pl.ds(0, fb)], wd_sem.at[0])
    wd_own.start()
    wd_sib = pltpu.make_async_remote_copy(
        src_ref=wd_stage.at[1 - c],
        dst_ref=wd_pair.at[:, pl.ds(fb, fb)],
        send_sem=wd_sem.at[1],
        recv_sem=wd_sem.at[2],
        device_id=sib,
        device_id_type=MESH,
    )
    wd_sib.start()
    wgx[:, pw:lanes, :] = jnp.zeros((n_pipe, lanes - pw, 2 * fb), BF)
    for j in range(2):
        everything = wgx.at[:, pl.ds(0, pw), pl.ds(j * fb, fb)]
        pltpu.make_async_copy(everything, everything, wload_sem.at[j]).wait()

    slot_id = iota((half, hslots), 1)
    target = (slot_id // SLOT) * cap + slot_id % SLOT
    pick = jnp.where(
        (iota((half, hslots), 0) == target) & (slot_id % SLOT < cap), 1.0, 0.0
    ).astype(BF)

    def block_of(rel):
        return 2 * ((y + rel + ny) % ny) + c

    def block_sib(rel):
        return 2 * ((y + rel + ny) % ny) + 1 - c

    def part_of(p, h):
        return xg.at[p, pl.ds(h * half, half)]

    def forward(way, d, h):
        sign = 1 if way == 0 else -1
        p = block_of(-sign * d)
        return pltpu.make_async_remote_copy(
            src_ref=part_of(p, h),
            dst_ref=part_of(p, h),
            send_sem=ag_ssem.at[way, d, h],
            recv_sem=ag_rsem.at[way, d, h],
            device_id=pipe_dev(sign),
            device_id_type=MESH,
        )

    def arrival(way, d, h):
        sign = 1 if way == 0 else -1
        p = block_of(-sign * d)
        return pltpu.make_async_remote_copy(
            src_ref=part_of(p, h),
            dst_ref=part_of(p, h),
            send_sem=ag_ssem.at[way, d - 1, h],
            recv_sem=ag_rsem.at[way, d - 1, h],
            device_id=pipe_dev(sign),
            device_id_type=MESH,
        )

    def to_sibling(rel, h):
        p = block_of(rel)
        return pltpu.make_async_remote_copy(
            src_ref=part_of(p, h),
            dst_ref=part_of(p, h),
            send_sem=sib_ssem.at[rel % ny, h],
            recv_sem=sib_rsem.at[rel % ny, h],
            device_id=sib,
            device_id_type=MESH,
        )

    def from_sibling(rel, h):
        p = block_sib(rel)
        return pltpu.make_async_remote_copy(
            src_ref=part_of(p, h),
            dst_ref=part_of(p, h),
            send_sem=sib_ssem.at[rel % ny, h],
            recv_sem=sib_rsem.at[rel % ny, h],
            device_id=sib,
            device_id_type=MESH,
        )

    def travels(way, d, h):
        return d < far - 1 or (d == far - 1 and h % 2 == way)

    sent = []

    def go(copy):
        copy.start()
        sent.append(copy)

    def gather_math(blocks, h=None, first=False):
        r = slice(0, rows) if h is None else slice(h * half, (h + 1) * half)
        total = None
        total_ss = None
        for p in blocks:
            one = dot(xg[p, r, :], wgx[p])
            ss = xg[p, r, lanes - 128 : lanes].astype(F32)
            total = one if total is None else total + one
            total_ss = ss if total_ss is None else total_ss + ss
        if first:
            acc[r, :] = total
            acc_ss[r, :] = total_ss
        else:
            acc[r, :] += total
            acc_ss[r, :] += total_ss

    def start_gather(h):
        here = group - 1 if h == self_turn else group
        if h == self_turn:
            own_block.wait()
        if here > 0:
            arrived = incoming.at[pl.ds(0, here)]
            pltpu.make_async_copy(arrived, arrived, disp_recv.at[h]).wait()
        flat = incoming[h * group : (h + 1) * group].reshape(hslots, lanes)
        me_block = block_of(0)
        xg[me_block, h * half : (h + 1) * half, :] = dot(pick, flat).astype(BF)
        for way in range(2):
            if travels(way, 0, h):
                go(forward(way, 0, h))
        go(to_sibling(0, h))

    def step_gather(d, h):
        for way in range(2):
            rel = -d if way == 0 else d
            arrival(way, d, h).wait_recv()
            if travels(way, d, h):
                go(forward(way, d, h))
            go(to_sibling(rel, h))

    def sibling_math(d):
        behind = [0] if d == 0 else [-d, d]
        for rel in behind:
            for h in range(turns):
                from_sibling(rel, h).wait_recv()
        gather_math([block_sib(rel) for rel in behind])

    def last_block(h):
        arrival(h % 2, far, h).wait_recv()
        go(to_sibling(far, h))
        gather_math([block_of(far)], h)

    def last_sibling_block(h):
        from_sibling(far, h).wait_recv()
        gather_math([block_sib(far)], h)

    first_spare = pw - (lanes - 128)

    def share_hidden(h):
        r = slice(h * half, (h + 1) * half)
        ss_lane = iota((half, 128), 1)
        ss = jnp.where((ss_lane >= first_spare) & (ss_lane < first_spare + 3), acc_ss[r, :], 0.0)
        scale = lax.rsqrt(jnp.sum(ss, axis=1, keepdims=True) / width + eps)
        gate = scale * acc[r, 0:fb]
        up = scale * acc[r, fb : 2 * fb]
        hidden = ((gate / (1.0 + jnp.exp(-gate))) * up).astype(BF)
        hid2[r, 0:fb] = hidden
        hid_own[r, :] = hidden
        copy = pltpu.make_async_remote_copy(
            src_ref=hid_own.at[pl.ds(h * half, half)],
            dst_ref=hid2.at[pl.ds(h * half, half), pl.ds(fb, fb)],
            send_sem=hid_ssem.at[h],
            recv_sem=hid_rsem.at[h],
            device_id=sib,
            device_id_type=MESH,
        )
        go(copy)
        return copy

    def contribution(rel, h):
        return dot(hid2[h * half : (h + 1) * half, :], wd_pair[(y + rel + ny) % ny])

    def pass_on(way, s, h):
        sign = 1 if way == 0 else -1
        return pltpu.make_async_remote_copy(
            src_ref=rst.at[way, s, h],
            dst_ref=rsr.at[way, s, h],
            send_sem=rs_ssem.at[way, s, h],
            recv_sem=rs_rsem.at[way, s, h],
            device_id=pipe_dev(sign),
            device_id_type=MESH,
        )

    def add_and_pass(way, s, h, adds):
        total = contribution((far - s) * (1 if way == 0 else -1), h)
        if adds:
            pass_on(way, s - 1, h).wait_recv()
            total = total + rsr[way, s - 1, h].astype(F32)
        rst[way, s, h] = total.astype(BF)
        go(pass_on(way, s, h))

    def start_scatter(h):
        add_and_pass(h % 2, 0, h, False)
        if far > 1:
            add_and_pass(1 - h % 2, 1, h, False)

    def step_scatter(s, h):
        add_and_pass(h % 2, s, h, True)
        if s + 1 < far:
            add_and_pass(1 - h % 2, s + 1, h, True)

    spread = (iota((hslots, half), 0) // SLOT) * cap + iota((hslots, half), 0) % SLOT
    unpick = jnp.where(
        (iota((hslots, half), 1) == spread) & (iota((hslots, half), 0) % SLOT < cap), 1.0, 0.0
    ).astype(BF)

    def give_back(i, _):
        pltpu.make_async_remote_copy(
            src_ref=ret_out.at[i],
            dst_ref=ret_in.at[me_e],
            send_sem=ret_send,
            recv_sem=ret_recv,
            device_id={"expert": source_of(i)},
            device_id_type=MESH,
        ).start()
        return 0

    own_back = pltpu.make_async_copy(ret_out.at[self_step], ret_in.at[me_e], ret_own)

    def end_scatter(h):
        total = contribution(0, h)
        for way in range(2):
            if far > 1 or h % 2 == way:
                pass_on(way, far - 1, h).wait_recv()
                total = total + rsr[way, far - 1, h].astype(F32)
        ret_out[h * group : (h + 1) * group] = (
            dot(unpick, total.astype(BF)).astype(BF).reshape(group, SLOT, lanes)
        )
        each_step(h * group, (h + 1) * group, give_back)
        if h == self_turn:
            own_back.start()

    for h in range(turns):
        start_gather(h)
    gather_math([block_of(0)], first=True)
    sibling_math(0)
    for d in range(1, far):
        for h in range(turns):
            step_gather(d, h)
        gather_math([block_of(-d), block_of(d)])
        sibling_math(d)
    wd_own.wait()
    wd_sib.wait()
    hid_copies = []
    last_block(0)
    last_block(1)
    for h in range(turns):
        last_sibling_block(h)
        hid_copies.append(share_hidden(h))
        if h + 2 < turns:
            last_block(h + 2)
        if h > 0:
            hid_copies[h - 1].wait_recv()
            start_scatter(h - 1)
    hid_copies[turns - 1].wait_recv()
    start_scatter(turns - 1)
    for t in range(1, far):
        for h in range(turns):
            step_scatter(t, h)
    for h in range(turns):
        end_scatter(h)

    others = lg_recv.at[pl.ds(0, n_pipe - 1)]
    pltpu.make_async_copy(others, others, lg_rsem).wait()
    sums = jnp.sum(lg_recv[...], axis=0)
    rstd = lax.rsqrt(sums[topk : topk + 1, :] / width + eps)
    scores = []
    for k in range(topk):
        logit = rstd * sums[k : k + 1, :]
        small = jnp.exp(-jnp.abs(logit))
        scores.append(jnp.where(logit >= 0, 1.0, small) / (1.0 + small))
    norm = scores[0]
    for k in range(1, topk):
        norm = norm + scores[k]
    weighted = jnp.zeros((slots, tok), F32)
    for k in range(topk):
        weighted = jnp.where(routes[k : k + 1, :] == expert_of, scores[k] / norm, weighted)
    weighted = weighted * place[...]
    w_hi = weighted.astype(BF)
    w_lo = (weighted - w_hi.astype(F32)).astype(BF)
    w_both = jnp.concatenate([w_hi, w_lo], axis=1)

    for copy in sent:
        copy.wait_send()
    block63 = outgoing.at[pl.ds(0, n_exp - 1)]
    pltpu.make_async_copy(block63, block63, disp_send).wait()
    sent15 = lg_recv.at[pl.ds(0, n_pipe - 1)]
    pltpu.make_async_copy(sent15, sent15, lg_ssem).wait()

    own_back.wait()
    back63 = ret_in.at[pl.ds(0, n_exp - 1)]
    pltpu.make_async_copy(back63, back63, ret_recv).wait()
    got = ret_in[...].reshape(slots, lanes)
    both = dot(got, w_both, 0, 0)
    out_ref[...] = (both[0:pw, 0:tok] + both[0:pw, tok : 2 * tok]).astype(BF)
    left63 = ret_out.at[pl.ds(0, n_exp - 1)]
    pltpu.make_async_copy(left63, left63, ret_send).wait()


def body(tokens, routes, router, w_gate, w_up, w_down):
    tok, pw = tokens.shape
    topk = routes.shape[1]
    n_exp = lax.axis_size("expert")
    n_pipe = lax.axis_size("pipe")
    cap = max(2, tok * topk // n_exp + max(1, tok * topk // (4 * n_exp)))
    width = pw * n_pipe
    lanes = -(-(pw + 3) // 128) * 128
    fb = w_gate.shape[2]
    ny = n_pipe // 2
    far = ny // 2
    rows = n_exp * cap
    nx = 8 if n_exp % 8 == 0 else n_exp
    turns = 4 if n_exp % 4 == 0 else 2
    cfg = (n_pipe, n_exp, nx, tok, topk, cap, pw, width, turns)
    dma = pltpu.SemaphoreType.DMA
    scratch = [
        pltpu.VMEM((lanes, tok), BF),
        pltpu.VMEM((topk, tok), jnp.int32),
        pltpu.VMEM((n_exp, pw), BF),
        pltpu.VMEM((n_pipe, lanes, 2 * fb), BF),
        pltpu.VMEM((fb, width), BF),
        pltpu.VMEM((2, ny, fb, lanes), BF),
        pltpu.VMEM((ny, 2 * fb, lanes), BF),
        pltpu.VMEM((n_exp * SLOT, tok), F32),
        pltpu.VMEM((n_exp, SLOT, lanes), BF),
        pltpu.VMEM((n_exp, SLOT, lanes), BF),
        pltpu.VMEM((n_pipe, rows, lanes), BF),
        pltpu.VMEM((rows, 2 * fb), F32),
        pltpu.VMEM((rows, 128), F32),
        pltpu.VMEM((rows, 2 * fb), BF),
        pltpu.VMEM((rows, fb), BF),
        pltpu.VMEM((2, far, turns, rows // turns, lanes), BF),
        pltpu.VMEM((2, far, turns, rows // turns, lanes), BF),
        pltpu.VMEM((n_exp, SLOT, lanes), BF),
        pltpu.VMEM((n_exp, SLOT, lanes), BF),
        pltpu.VMEM((8, tok), F32),
        pltpu.VMEM((n_pipe, 8, tok), F32),
        dma((4,)),
        dma((2,)),
        dma,
        dma((turns,)),
        dma,
        dma,
        dma,
        dma((3,)),
        dma((2, far, turns)),
        dma((2, far, turns)),
        dma((ny, turns)),
        dma((ny, turns)),
        dma((turns,)),
        dma((turns,)),
        dma((2, far, turns)),
        dma((2, far, turns)),
        dma,
        dma,
        dma,
    ]
    mixed = pl.pallas_call(
        functools.partial(kernel, cfg),
        out_shape=jax.ShapeDtypeStruct((pw, tok), BF),
        in_specs=[pl.BlockSpec(memory_space=pl.ANY)] * 6,
        out_specs=pl.BlockSpec(memory_space=pltpu.VMEM),
        scratch_shapes=scratch,
        compiler_params=pltpu.CompilerParams(
            collective_id=0, has_side_effects=True, vmem_limit_bytes=60 << 20
        ),
    )(tokens.T, routes.T, router.T, w_gate, w_up, w_down)
    return mixed.T


def solution(mesh):
    placed = (
        P("expert", "pipe"),
        P("expert", None),
        P("pipe", None),
        P("expert", None, "pipe"),
        P("expert", None, "pipe"),
        P("expert", "pipe", None),
    )
    return jax.shard_map(
        body, mesh=mesh, in_specs=placed, out_specs=P("expert", "pipe"), check_vma=False
    )
```

```python
import functools

import jax
import jax.numpy as jnp
from jax import lax
from jax.experimental import pallas as pl
from jax.experimental.pallas import tpu as pltpu
from jax.sharding import PartitionSpec as P

eps = 1e-06
MESH = pl.DeviceIdType.MESH
BF = jnp.bfloat16
F32 = jnp.float32
SLOT = 8


def dot(a, b, ca=1, cb=0):
    return lax.dot_general(a, b, (((ca,), (cb,)), ((), ())), preferred_element_type=F32)


def iota(shape, axis):
    return lax.broadcasted_iota(jnp.int32, shape, axis)


def kernel(
    cfg,
    tok_hbm,
    routes_hbm,
    router_hbm,
    wg_hbm,
    wu_hbm,
    wd_hbm,
    out_ref,
    tokx,
    routes,
    router,
    wgx,
    wd_raw,
    wd_stage,
    wd_pair,
    place,
    outgoing,
    incoming,
    xg,
    acc,
    acc_ss,
    hid2,
    hid_own,
    rst,
    rsr,
    ret_out,
    ret_in,
    lg_send,
    lg_recv,
    load_sem,
    wload_sem,
    disp_send,
    disp_recv,
    disp_own,
    lg_ssem,
    lg_rsem,
    wd_sem,
    ag_ssem,
    ag_rsem,
    sib_ssem,
    sib_rsem,
    hid_ssem,
    hid_rsem,
    rs_ssem,
    rs_rsem,
    ret_send,
    ret_recv,
    ret_own,
):
    n_pipe, n_exp, nx, tok, topk, cap, pw, width, turns = cfg
    ny = n_pipe // 2
    far = ny // 2
    nz = n_exp // nx
    lanes = xg.shape[2]
    fb = wd_raw.shape[0]
    rows = n_exp * cap
    half = rows // turns
    slots = n_exp * SLOT
    hslots = slots // turns
    group = n_exp // turns
    me_p = lax.axis_index("pipe")
    me_e = lax.axis_index("expert")
    y = me_p // 2
    c = me_p % 2
    ez = me_e // nx
    ex = me_e % nx

    def offset(i):
        if nz < 4:
            return 0, i % nx
        row, col = nz - 1 - i // nx, i % nx
        dz = jnp.where(row % 2 == 1, (row + 1) // 2, nz - (row + 1) // 2)
        return dz, col + nx // 2

    self_step = 0 if nz < 4 else (nz - 1) * nx + nx // 2
    self_turn = self_step // group

    def peer_of(i):
        dz, dx = offset(i)
        return ((ez + dz) % nz) * nx + (ex + dx) % nx

    def source_of(i):
        dz, dx = offset(i)
        return ((ez + 2 * nz - dz) % nz) * nx + (ex + 2 * nx - dx) % nx

    def each_step(low, high, do):
        if low <= self_step < high:
            lax.fori_loop(low, self_step, do, 0)
            lax.fori_loop(self_step + 1, high, do, 0)
        else:
            lax.fori_loop(low, high, do, 0)

    def pipe_dev(rel):
        return {"pipe": 2 * ((y + rel + ny) % ny) + c}

    sib = {"pipe": 2 * y + 1 - c}

    load_tok = pltpu.make_async_copy(tok_hbm, tokx.at[pl.ds(0, pw)], load_sem.at[0])
    load_routes = pltpu.make_async_copy(routes_hbm, routes, load_sem.at[1])
    load_router = pltpu.make_async_copy(router_hbm, router, load_sem.at[2])
    load_wd = pltpu.make_async_copy(wd_hbm.at[0], wd_raw, load_sem.at[3])
    load_tok.start()
    load_routes.start()
    load_router.start()
    load_wd.start()

    barrier = pltpu.get_barrier_semaphore()

    def greet_expert(i, _):
        pl.semaphore_signal(barrier, inc=1, device_id={"expert": peer_of(i)}, device_id_type=MESH)
        return 0

    def greet_pipe(i, _):
        pl.semaphore_signal(
            barrier, inc=1, device_id={"pipe": (me_p + i) % n_pipe}, device_id_type=MESH
        )
        return 0

    each_step(0, n_exp, greet_expert)
    lax.fori_loop(1, n_pipe, greet_pipe, 0)

    def load_w(p, _):
        src = pl.ds(pl.multiple_of(p * pw, 16), pw)
        pltpu.make_async_copy(
            wg_hbm.at[0, src], wgx.at[p, pl.ds(0, pw), pl.ds(0, fb)], wload_sem.at[0]
        ).start()
        pltpu.make_async_copy(
            wu_hbm.at[0, src], wgx.at[p, pl.ds(0, pw), pl.ds(fb, fb)], wload_sem.at[1]
        ).start()
        return 0

    lax.fori_loop(0, n_pipe, load_w, 0)

    load_routes.wait()
    expert_of = iota((slots, tok), 0) // SLOT
    slot_of = (iota((slots, tok), 0) % SLOT).astype(F32)
    named = jnp.where(routes[0:1, :] == expert_of, 1.0, 0.0)
    for k in range(1, topk):
        named = named + jnp.where(routes[k : k + 1, :] == expert_of, 1.0, 0.0)
    earlier = jnp.where(iota((tok, tok), 0) < iota((tok, tok), 1), 1.0, 0.0).astype(BF)
    count = dot(named.astype(BF), earlier)
    placed = jnp.where(count == slot_of, named, 0.0)
    place[...] = placed

    load_tok.wait()
    tf = tokx[0:pw, :].astype(F32)
    square = jnp.sum(tf * tf, axis=0, keepdims=True)
    hi = square.astype(BF).astype(F32)
    mid = (square - hi).astype(BF).astype(F32)
    lo = square - hi - mid
    spare = iota((lanes - pw, tok), 0)
    tokx[pw:lanes, :] = jnp.where(
        spare == 0, hi, jnp.where(spare == 1, mid, jnp.where(spare == 2, lo, 0.0))
    ).astype(BF)
    outgoing[...] = (
        dot(placed.astype(BF), tokx[...], 1, 1).astype(BF).reshape(n_exp, SLOT, lanes)
    )

    pl.semaphore_wait(barrier, n_exp - 1 + n_pipe - 1)

    def dispatch(i, _):
        dest = peer_of(i)
        pltpu.make_async_remote_copy(
            src_ref=outgoing.at[dest],
            dst_ref=incoming.at[i],
            send_sem=disp_send,
            recv_sem=disp_recv.at[i // group],
            device_id={"expert": dest},
            device_id_type=MESH,
        ).start()
        return 0

    own_block = pltpu.make_async_copy(outgoing.at[me_e], incoming.at[self_step], disp_own)
    own_block.start()
    each_step(0, n_exp, dispatch)

    load_router.wait()
    part = dot(router[...], tokx[0:pw, :])
    picks = []
    for k in range(topk):
        picks.append(
            jnp.sum(
                jnp.where(iota((n_exp, tok), 0) == routes[k : k + 1, :], part, 0.0),
                axis=0,
                keepdims=True,
            )
        )
    row8 = iota((8, tok), 0)
    packed = jnp.where(row8 == topk, square, 0.0)
    for k in range(topk):
        packed = jnp.where(row8 == k, picks[k], packed)
    lg_send[...] = packed
    lg_recv[pl.ds(me_p, 1)] = packed[None]

    def send_logits(i, _):
        pltpu.make_async_remote_copy(
            src_ref=lg_send,
            dst_ref=lg_recv.at[me_p],
            send_sem=lg_ssem,
            recv_sem=lg_rsem,
            device_id={"pipe": (me_p + i) % n_pipe},
            device_id_type=MESH,
        ).start()
        return 0

    lax.fori_loop(1, n_pipe, send_logits, 0)

    load_wd.wait()
    for p in range(n_pipe):
        base = (pw * p) // 128 * 128
        off = pw * p - base
        span = min(-(-(off + pw) // 128) * 128, wd_raw.shape[1] - base)
        shift = (iota((span, lanes), 0) == iota((span, lanes), 1) + off) & (
            iota((span, lanes), 1) < pw
        )
        wd_stage[p % 2, p // 2] = dot(
            wd_raw[:, base : base + span], jnp.where(shift, 1.0, 0.0).astype(BF)
        ).astype(BF)
    wd_own = pltpu.make_async_copy(wd_stage.at[c], wd_pair.at[:, pl.ds(0, fb)], wd_sem.at[0])
    wd_own.start()
    wd_sib = pltpu.make_async_remote_copy(
        src_ref=wd_stage.at[1 - c],
        dst_ref=wd_pair.at[:, pl.ds(fb, fb)],
        send_sem=wd_sem.at[1],
        recv_sem=wd_sem.at[2],
        device_id=sib,
        device_id_type=MESH,
    )
    wd_sib.start()
    wgx[:, pw:lanes, :] = jnp.zeros((n_pipe, lanes - pw, 2 * fb), BF)
    for j in range(2):
        everything = wgx.at[:, pl.ds(0, pw), pl.ds(j * fb, fb)]
        pltpu.make_async_copy(everything, everything, wload_sem.at[j]).wait()

    slot_id = iota((half, hslots), 1)
    target = (slot_id // SLOT) * cap + slot_id % SLOT
    pick = jnp.where(
        (iota((half, hslots), 0) == target) & (slot_id % SLOT < cap), 1.0, 0.0
    ).astype(BF)

    def block_of(rel):
        return 2 * ((y + rel + ny) % ny) + c

    def block_sib(rel):
        return 2 * ((y + rel + ny) % ny) + 1 - c

    def part_of(p, h):
        return xg.at[p, pl.ds(h * half, half)]

    def forward(way, d, h):
        sign = 1 if way == 0 else -1
        p = block_of(-sign * d)
        return pltpu.make_async_remote_copy(
            src_ref=part_of(p, h),
            dst_ref=part_of(p, h),
            send_sem=ag_ssem.at[way, d, h],
            recv_sem=ag_rsem.at[way, d, h],
            device_id=pipe_dev(sign),
            device_id_type=MESH,
        )

    def arrival(way, d, h):
        sign = 1 if way == 0 else -1
        p = block_of(-sign * d)
        return pltpu.make_async_remote_copy(
            src_ref=part_of(p, h),
            dst_ref=part_of(p, h),
            send_sem=ag_ssem.at[way, d - 1, h],
            recv_sem=ag_rsem.at[way, d - 1, h],
            device_id=pipe_dev(sign),
            device_id_type=MESH,
        )

    def to_sibling(rel, h):
        p = block_of(rel)
        return pltpu.make_async_remote_copy(
            src_ref=part_of(p, h),
            dst_ref=part_of(p, h),
            send_sem=sib_ssem.at[rel % ny, h],
            recv_sem=sib_rsem.at[rel % ny, h],
            device_id=sib,
            device_id_type=MESH,
        )

    def from_sibling(rel, h):
        p = block_sib(rel)
        return pltpu.make_async_remote_copy(
            src_ref=part_of(p, h),
            dst_ref=part_of(p, h),
            send_sem=sib_ssem.at[rel % ny, h],
            recv_sem=sib_rsem.at[rel % ny, h],
            device_id=sib,
            device_id_type=MESH,
        )

    def travels(way, d, h):
        return d < far - 1 or (d == far - 1 and h % 2 == way)

    sent = []

    def go(copy):
        copy.start()
        sent.append(copy)

    def gather_math(blocks, h=None, first=False):
        r = slice(0, rows) if h is None else slice(h * half, (h + 1) * half)
        total = None
        total_ss = None
        for p in blocks:
            one = dot(xg[p, r, :], wgx[p])
            ss = xg[p, r, lanes - 128 : lanes].astype(F32)
            total = one if total is None else total + one
            total_ss = ss if total_ss is None else total_ss + ss
        if first:
            acc[r, :] = total
            acc_ss[r, :] = total_ss
        else:
            acc[r, :] += total
            acc_ss[r, :] += total_ss

    def start_gather(h):
        here = group - 1 if h == self_turn else group
        if h == self_turn:
            own_block.wait()
        if here > 0:
            arrived = incoming.at[pl.ds(0, here)]
            pltpu.make_async_copy(arrived, arrived, disp_recv.at[h]).wait()
        flat = incoming[h * group : (h + 1) * group].reshape(hslots, lanes)
        me_block = block_of(0)
        xg[me_block, h * half : (h + 1) * half, :] = dot(pick, flat).astype(BF)
        for way in range(2):
            if travels(way, 0, h):
                go(forward(way, 0, h))
        go(to_sibling(0, h))

    def step_gather(d, h):
        for way in range(2):
            rel = -d if way == 0 else d
            arrival(way, d, h).wait_recv()
            if travels(way, d, h):
                go(forward(way, d, h))
            go(to_sibling(rel, h))

    def sibling_math(d):
        behind = [0] if d == 0 else [-d, d]
        for rel in behind:
            for h in range(turns):
                from_sibling(rel, h).wait_recv()
        gather_math([block_sib(rel) for rel in behind])

    def last_block(h):
        arrival(h % 2, far, h).wait_recv()
        go(to_sibling(far, h))
        gather_math([block_of(far)], h)

    def last_sibling_block(h):
        from_sibling(far, h).wait_recv()
        gather_math([block_sib(far)], h)

    first_spare = pw - (lanes - 128)

    def share_hidden(h):
        r = slice(h * half, (h + 1) * half)
        ss_lane = iota((half, 128), 1)
        ss = jnp.where((ss_lane >= first_spare) & (ss_lane < first_spare + 3), acc_ss[r, :], 0.0)
        scale = lax.rsqrt(jnp.sum(ss, axis=1, keepdims=True) / width + eps)
        gate = scale * acc[r, 0:fb]
        up = scale * acc[r, fb : 2 * fb]
        hidden = ((gate / (1.0 + jnp.exp(-gate))) * up).astype(BF)
        hid2[r, 0:fb] = hidden
        hid_own[r, :] = hidden
        copy = pltpu.make_async_remote_copy(
            src_ref=hid_own.at[pl.ds(h * half, half)],
            dst_ref=hid2.at[pl.ds(h * half, half), pl.ds(fb, fb)],
            send_sem=hid_ssem.at[h],
            recv_sem=hid_rsem.at[h],
            device_id=sib,
            device_id_type=MESH,
        )
        go(copy)
        return copy

    def contribution(rel, h):
        return dot(hid2[h * half : (h + 1) * half, :], wd_pair[(y + rel + ny) % ny])

    def pass_on(way, s, h):
        sign = 1 if way == 0 else -1
        return pltpu.make_async_remote_copy(
            src_ref=rst.at[way, s, h],
            dst_ref=rsr.at[way, s, h],
            send_sem=rs_ssem.at[way, s, h],
            recv_sem=rs_rsem.at[way, s, h],
            device_id=pipe_dev(sign),
            device_id_type=MESH,
        )

    def own_part(way, s, h):
        return contribution((far - s) * (1 if way == 0 else -1), h)

    def add_and_pass(way, s, h, adds, total):
        if adds:
            pass_on(way, s - 1, h).wait_recv()
            total = total + rsr[way, s - 1, h].astype(F32)
        rst[way, s, h] = total.astype(BF)
        go(pass_on(way, s, h))

    def start_scatter(h):
        add_and_pass(h % 2, 0, h, False, own_part(h % 2, 0, h))
        if far > 1:
            add_and_pass(1 - h % 2, 1, h, False, own_part(1 - h % 2, 1, h))

    def own_parts(s, h):
        late = own_part(1 - h % 2, s + 1, h) if s + 1 < far else None
        return own_part(h % 2, s, h), late

    def step_scatter(s, h, own):
        add_and_pass(h % 2, s, h, True, own[0])
        if s + 1 < far:
            add_and_pass(1 - h % 2, s + 1, h, True, own[1])

    spread = (iota((hslots, half), 0) // SLOT) * cap + iota((hslots, half), 0) % SLOT
    unpick = jnp.where(
        (iota((hslots, half), 1) == spread) & (iota((hslots, half), 0) % SLOT < cap), 1.0, 0.0
    ).astype(BF)

    def give_back(i, _):
        pltpu.make_async_remote_copy(
            src_ref=ret_out.at[i],
            dst_ref=ret_in.at[me_e],
            send_sem=ret_send,
            recv_sem=ret_recv,
            device_id={"expert": source_of(i)},
            device_id_type=MESH,
        ).start()
        return 0

    own_back = pltpu.make_async_copy(ret_out.at[self_step], ret_in.at[me_e], ret_own)

    def end_scatter(h, total):
        for way in range(2):
            if far > 1 or h % 2 == way:
                pass_on(way, far - 1, h).wait_recv()
                total = total + rsr[way, far - 1, h].astype(F32)
        ret_out[h * group : (h + 1) * group] = (
            dot(unpick, total.astype(BF)).astype(BF).reshape(group, SLOT, lanes)
        )
        each_step(h * group, (h + 1) * group, give_back)
        if h == self_turn:
            own_back.start()

    for h in range(turns):
        start_gather(h)
    gather_math([block_of(0)], first=True)
    sibling_math(0)
    for d in range(1, far):
        for h in range(turns):
            step_gather(d, h)
        gather_math([block_of(-d), block_of(d)])
        sibling_math(d)
    wd_own.wait()
    wd_sib.wait()
    hid_copies = []
    last_block(0)
    last_block(1)
    for h in range(turns):
        last_sibling_block(h)
        hid_copies.append(share_hidden(h))
        if h + 2 < turns:
            last_block(h + 2)
        if h > 0:
            hid_copies[h - 1].wait_recv()
            start_scatter(h - 1)
    hid_copies[turns - 1].wait_recv()
    start_scatter(turns - 1)
    for t in range(1, far):
        own = [own_parts(t, h) for h in range(turns)]
        for h in range(turns):
            step_scatter(t, h, own[h])
    own = [contribution(0, h) for h in range(turns)]
    for h in range(turns):
        end_scatter(h, own[h])

    others = lg_recv.at[pl.ds(0, n_pipe - 1)]
    pltpu.make_async_copy(others, others, lg_rsem).wait()
    sums = jnp.sum(lg_recv[...], axis=0)
    rstd = lax.rsqrt(sums[topk : topk + 1, :] / width + eps)
    scores = []
    for k in range(topk):
        logit = rstd * sums[k : k + 1, :]
        small = jnp.exp(-jnp.abs(logit))
        scores.append(jnp.where(logit >= 0, 1.0, small) / (1.0 + small))
    norm = scores[0]
    for k in range(1, topk):
        norm = norm + scores[k]
    weighted = jnp.zeros((slots, tok), F32)
    for k in range(topk):
        weighted = jnp.where(routes[k : k + 1, :] == expert_of, scores[k] / norm, weighted)
    weighted = weighted * place[...]
    w_hi = weighted.astype(BF)
    w_lo = (weighted - w_hi.astype(F32)).astype(BF)
    w_both = jnp.concatenate([w_hi, w_lo], axis=1).T

    for copy in sent:
        copy.wait_send()
    block63 = outgoing.at[pl.ds(0, n_exp - 1)]
    pltpu.make_async_copy(block63, block63, disp_send).wait()
    sent15 = lg_recv.at[pl.ds(0, n_pipe - 1)]
    pltpu.make_async_copy(sent15, sent15, lg_ssem).wait()

    own_back.wait()
    back63 = ret_in.at[pl.ds(0, n_exp - 1)]
    pltpu.make_async_copy(back63, back63, ret_recv).wait()
    got = ret_in[...].reshape(slots, lanes)
    both = dot(w_both, got)
    out_ref[...] = (both[0:tok] + both[tok : 2 * tok]).T[0:pw, :].astype(BF)
    left63 = ret_out.at[pl.ds(0, n_exp - 1)]
    pltpu.make_async_copy(left63, left63, ret_send).wait()


def body(tokens, routes, router, w_gate, w_up, w_down):
    tok, pw = tokens.shape
    topk = routes.shape[1]
    n_exp = lax.axis_size("expert")
    n_pipe = lax.axis_size("pipe")
    cap = max(2, tok * topk // n_exp + max(1, tok * topk // (4 * n_exp)))
    width = pw * n_pipe
    lanes = -(-(pw + 3) // 128) * 128
    fb = w_gate.shape[2]
    ny = n_pipe // 2
    far = ny // 2
    rows = n_exp * cap
    nx = 8 if n_exp % 8 == 0 else n_exp
    turns = 4 if n_exp % 4 == 0 else 2
    cfg = (n_pipe, n_exp, nx, tok, topk, cap, pw, width, turns)
    dma = pltpu.SemaphoreType.DMA
    scratch = [
        pltpu.VMEM((lanes, tok), BF),
        pltpu.VMEM((topk, tok), jnp.int32),
        pltpu.VMEM((n_exp, pw), BF),
        pltpu.VMEM((n_pipe, lanes, 2 * fb), BF),
        pltpu.VMEM((fb, width), BF),
        pltpu.VMEM((2, ny, fb, lanes), BF),
        pltpu.VMEM((ny, 2 * fb, lanes), BF),
        pltpu.VMEM((n_exp * SLOT, tok), F32),
        pltpu.VMEM((n_exp, SLOT, lanes), BF),
        pltpu.VMEM((n_exp, SLOT, lanes), BF),
        pltpu.VMEM((n_pipe, rows, lanes), BF),
        pltpu.VMEM((rows, 2 * fb), F32),
        pltpu.VMEM((rows, 128), F32),
        pltpu.VMEM((rows, 2 * fb), BF),
        pltpu.VMEM((rows, fb), BF),
        pltpu.VMEM((2, far, turns, rows // turns, lanes), BF),
        pltpu.VMEM((2, far, turns, rows // turns, lanes), BF),
        pltpu.VMEM((n_exp, SLOT, lanes), BF),
        pltpu.VMEM((n_exp, SLOT, lanes), BF),
        pltpu.VMEM((8, tok), F32),
        pltpu.VMEM((n_pipe, 8, tok), F32),
        dma((4,)),
        dma((2,)),
        dma,
        dma((turns,)),
        dma,
        dma,
        dma,
        dma((3,)),
        dma((2, far, turns)),
        dma((2, far, turns)),
        dma((ny, turns)),
        dma((ny, turns)),
        dma((turns,)),
        dma((turns,)),
        dma((2, far, turns)),
        dma((2, far, turns)),
        dma,
        dma,
        dma,
    ]
    mixed = pl.pallas_call(
        functools.partial(kernel, cfg),
        out_shape=jax.ShapeDtypeStruct((pw, tok), BF),
        in_specs=[pl.BlockSpec(memory_space=pl.ANY)] * 6,
        out_specs=pl.BlockSpec(memory_space=pltpu.VMEM),
        scratch_shapes=scratch,
        compiler_params=pltpu.CompilerParams(
            collective_id=0, has_side_effects=True, vmem_limit_bytes=60 << 20
        ),
    )(tokens.T, routes.T, router.T, w_gate, w_up, w_down)
    return mixed.T


def solution(mesh):
    placed = (
        P("expert", "pipe"),
        P("expert", None),
        P("pipe", None),
        P("expert", None, "pipe"),
        P("expert", None, "pipe"),
        P("expert", "pipe", None),
    )
    return jax.shard_map(
        body, mesh=mesh, in_specs=placed, out_specs=P("expert", "pipe"), check_vma=False
    )
```
